32 devices in a mesh: img: 8 (over z, y), cap: 4 (over x, core).
Axes of the slice: x: 2, y: 2, z: 4, core: 2. Of those that a mesh axis runs over, the one named last changes fastest.
Arguments:
- tile_values: bfloat16 [5120, 512, 128], P('img', 'cap'), may hold values from -0.078125 to 0.078125
- tile_rows: int32 [8, 2560], P('img', 'cap'), may hold values from 0 to 63, as said below
- tile_cols: int32 [8, 2560], P('img', 'cap'), may hold values from 0 to 63
- tile_count: int32 [8, 4], P('img', 'cap'), may hold values from 81 to 640, as said below
- row_degree: float32 [65536], P('img'), may hold values from 1 to 10
- col_degree: float32 [32768], P('cap'), may hold values from 1 to 10
- start_panel: bfloat16 [32768, 128], P('cap'), may hold values from -6 to 6
Outputs:
- basis: float32 [65536, 128], P(('img', 'cap'))
- factor: float32 [128, 128], replicated
- next_panel: bfloat16 [32768, 128], P('cap')
The draws below stay inside these ranges and needn't reach their ends.
Inputs may be any that keep to these rules, and one draw needn't show every extreme that they name: `tile_rows`: tile rows lie in 0 to 63; within one device's slots no (tile row, tile column) pair repeats. Only the first tile_count slots of a device are live; some device has all 640 slots live.
All inputs are finite; a program needn't handle non-finite values.
Results may differ from the reference program's by a relative error of at most 0.007.
Values may be sent and summed in bfloat16 or wider, within the bound.
No kernel may reach another device: no remote copies, remote signals or barrier semaphores. Data moves between devices by JAX's collectives and lax.ppermute only.
A program may use at most 256 MiB of HBM per device.

```python
import math
import jax
import jax.numpy as jnp
from jax import lax

K = 128
TILE = 128
ROWS_DEV = 8192
COLS_DEV = 8192
TILES_DEV = 640
ROW_TILES = 64
COL_TILES = 64
IMAGES = 65536
CAPTIONS = 32768
N_IMG = 8
N_CAP = 4


def tile_positions(key):
    keys = jax.random.split(key, N_IMG * N_CAP)
    chosen = jax.vmap(lambda one: jax.random.permutation(one, ROW_TILES * COL_TILES)[:TILES_DEV])(keys)
    return chosen.reshape(N_IMG, N_CAP * TILES_DEV).astype(jnp.int32)


def draw_tile_rows(key, part):
    positions = tile_positions(key)
    return (positions // COL_TILES).astype(jnp.int32)


def draw_tile_cols(key, part):
    positions = tile_positions(key)
    return (positions % COL_TILES).astype(jnp.int32)


def draw_tile_count(key, part):
    key = jax.random.fold_in(key, 7)
    first, second = jax.random.split(key)
    lowest = TILES_DEV // 8 + 1
    spread = jax.random.randint(first, (N_IMG, N_CAP), 0, 1001)
    counts = lowest + (TILES_DEV - lowest) * spread * spread // 1000000
    fullest = jax.random.randint(second, (), 0, N_IMG * N_CAP)
    places = jnp.arange(N_IMG * N_CAP, dtype=jnp.int32).reshape(N_IMG, N_CAP)
    return jnp.where(places == fullest, TILES_DEV, counts).astype(jnp.int32)


def level_of(own_key, shape, shards, low, top_value):
    def one(axis_at, shards_of):
        draws = jax.random.uniform(jax.random.fold_in(jax.random.fold_in(own_key, 6), axis_at), (shards_of,), jnp.float32, low / len(shards), top_value / len(shards))
        return jnp.repeat(jnp.exp(draws), shape[axis_at] // shards_of).reshape((-1,) + (1,) * (len(shape) - axis_at - 1))

    gain = one(*shards[0])
    for cut in shards[1:]:
        gain = gain * one(*cut)
    return gain


def bell_draw(stream_key, extent, scale, limit, cuts=(), kind=jnp.bfloat16):
    result = scale * jax.random.normal(stream_key, extent, jnp.float32)
    if cuts:
        result = result * level_of(stream_key, extent, cuts, -0.22, 0.18)
    return jnp.clip(result, -limit, limit).astype(kind)


def setup_inputs(seed: int = 0) -> dict:
    streams_of = jax.random.split(jax.random.key(seed), 8)
    return {
        "tile_values": bell_draw(streams_of[0], (N_IMG * TILES_DEV, N_CAP * TILE, TILE), (N_CAP * TILES_DEV * TILE * TILE // ROWS_DEV) ** -0.5, 0.078125, ((0, 8), (1, 4))),
        "tile_rows": draw_tile_rows(jax.random.fold_in(streams_of[7], 71), 0),
        "tile_cols": draw_tile_cols(jax.random.fold_in(streams_of[7], 71), 0),
        "tile_count": draw_tile_count(jax.random.fold_in(streams_of[7], 71), 0),
        "row_degree": jnp.clip(jnp.exp(math.log(10.0) - 2.3025851 * jax.random.uniform(streams_of[4], (IMAGES,), jnp.float32) ** level_of(streams_of[4], (IMAGES,), ((0, 8),), -0.2, 0.2)), 1.0, 10.0),
        "col_degree": jnp.clip(jnp.exp(math.log(10.0) - 2.3025851 * jax.random.uniform(streams_of[5], (CAPTIONS,), jnp.float32) ** level_of(streams_of[5], (CAPTIONS,), ((0, 4),), -0.2, 0.2)), 1.0, 10.0),
        "start_panel": bell_draw(streams_of[6], (CAPTIONS, K), 1.0, 6.0, ((0, 4),)),
    }


def forward_block(tiles, rows, cols, count, panel):
    gathered = panel.reshape(COL_TILES, TILE, K)[cols]
    product = jnp.einsum('tbc,tck->tbk', tiles.astype(jnp.float32), gathered.astype(jnp.float32), precision=lax.Precision.HIGHEST)
    live = jnp.arange(TILES_DEV, dtype=jnp.int32) < count
    select = ((rows[None, :] == jnp.arange(ROW_TILES, dtype=jnp.int32)[:, None]) & live[None, :]).astype(jnp.float32)
    summed = jnp.dot(select.astype(jnp.float32), product.reshape(TILES_DEV, TILE * K).astype(jnp.float32), precision=lax.Precision.HIGHEST, preferred_element_type=jnp.float32)
    return summed.reshape(ROWS_DEV, K)

def backward_block(tiles, rows, cols, count, panel):
    gathered = panel.reshape(ROW_TILES, TILE, K)[rows]
    product = jnp.einsum('tbc,tbk->tck', tiles.astype(jnp.float32), gathered.astype(jnp.float32), precision=lax.Precision.HIGHEST)
    live = jnp.arange(TILES_DEV, dtype=jnp.int32) < count
    select = ((cols[None, :] == jnp.arange(COL_TILES, dtype=jnp.int32)[:, None]) & live[None, :]).astype(jnp.float32)
    summed = jnp.dot(select.astype(jnp.float32), product.reshape(TILES_DEV, TILE * K).astype(jnp.float32), precision=lax.Precision.HIGHEST, preferred_element_type=jnp.float32)
    return summed.reshape(COLS_DEV, K)

def block_of(tile_values, tile_rows, tile_cols, tile_count, row_at, col_at):
    tiles = lax.dynamic_slice(tile_values, (row_at * TILES_DEV, col_at * TILE, jnp.int32(0)), (TILES_DEV, TILE, TILE))
    rows = lax.dynamic_slice(tile_rows, (row_at, col_at * TILES_DEV), (1, TILES_DEV))[0]
    cols = lax.dynamic_slice(tile_cols, (row_at, col_at * TILES_DEV), (1, TILES_DEV))[0]
    count = lax.dynamic_slice(tile_count, (row_at, col_at), (1, 1))[0, 0]
    return (tiles, rows, cols, count)

def reference(tile_values, tile_rows, tile_cols, tile_count, row_degree, col_degree, start_panel):
    row_scale = 1.0 / jnp.sqrt(row_degree)
    col_scale = 1.0 / jnp.sqrt(col_degree)
    scaled_start = (start_panel.astype(jnp.float32) * col_scale[:, None]).astype(jnp.bfloat16)

    def image_block(row_at):

        def add_col(col_at, total):
            col_at = col_at.astype(jnp.int32)
            tiles, rows, cols, count = block_of(tile_values, tile_rows, tile_cols, tile_count, row_at, col_at)
            panel = lax.dynamic_slice_in_dim(scaled_start, col_at * COLS_DEV, COLS_DEV, 0)
            return total + forward_block(tiles, rows, cols, count, panel)
        return lax.fori_loop(jnp.int32(0), jnp.int32(N_CAP), add_col, jnp.zeros((ROWS_DEV, K), jnp.float32))
    sums = lax.map(image_block, jnp.arange(N_IMG, dtype=jnp.int32)).reshape(IMAGES, K)
    image_panel = sums * row_scale[:, None]
    ortho, upper = jnp.linalg.qr(image_panel)
    signs = jnp.sign(jnp.diagonal(upper))
    root = math.sqrt(IMAGES)
    basis = ortho * signs[None, :] * root
    factor = upper * signs[:, None] / root
    scaled_image = (image_panel * row_scale[:, None]).astype(jnp.bfloat16)

    def caption_block(col_at):

        def add_row(row_at, total):
            row_at = row_at.astype(jnp.int32)
            tiles, rows, cols, count = block_of(tile_values, tile_rows, tile_cols, tile_count, row_at, col_at)
            panel = lax.dynamic_slice_in_dim(scaled_image, row_at * ROWS_DEV, ROWS_DEV, 0)
            return total + backward_block(tiles, rows, cols, count, panel)
        return lax.fori_loop(jnp.int32(0), jnp.int32(N_IMG), add_row, jnp.zeros((COLS_DEV, K), jnp.float32))
    caption_sums = lax.map(caption_block, jnp.arange(N_CAP, dtype=jnp.int32)).reshape(CAPTIONS, K)
    next_panel = (caption_sums * col_scale[:, None]).astype(jnp.bfloat16)
    return (basis, factor, next_panel)
```

```python
import functools
import math

import jax
import jax.numpy as jnp
from jax import lax
from jax.experimental import pallas as pl
from jax.experimental.pallas import tpu as pltpu
from jax.sharding import PartitionSpec as P

F32 = jnp.float32
BF16 = jnp.bfloat16


def swap(x, axis, bit):
    n = lax.axis_size(axis)
    return lax.ppermute(x, axis, [(i, i ^ (1 << bit)) for i in range(n)])


def bit_of(axis, bit):
    return (lax.axis_index(axis) >> bit) & 1


def accumulate(transposed, step, unroll, count, src, dst, tiles, panel, accs):
    g = pl.program_id(0)
    dead = accs[0].shape[0] - 1

    @pl.when(g == 0)
    def _():
        for acc in accs:
            acc[...] = jnp.zeros_like(acc)

    dims = (((0,), (0,)), ((), ())) if transposed else (((1,), (0,)), ((), ()))

    def group(u, carry):
        for j in range(unroll):
            t = u * unroll + j
            s = g * step + t
            to = jnp.where(s < count, dst[s], dead)
            accs[j % len(accs)][to] += lax.dot_general(
                tiles[t], panel[src[s]], dims, preferred_element_type=F32
            )
        return carry

    groups = jnp.clip(pl.cdiv(count - g * step, unroll), 0, step // unroll)
    lax.fori_loop(0, groups, group, 0)


def total(accs, at):
    value = accs[0][at]
    for acc in accs[1:]:
        value = value + acc[at]
    return value


def forward_kernel(step, unroll, src, dst, meta, tiles, panel, own, send, *accs):
    accumulate(False, step, unroll, meta[0], src, dst, tiles, panel, accs)

    @pl.when(pl.program_id(0) == pl.num_programs(0) - 1)
    def _():
        core = meta[1]
        shares, share = own.shape[0], own.shape[1]
        for h in range(shares):

            def block(i, carry):
                own[h, i] = total(accs, (2 * h + core) * share + i)
                send[h, i] = total(accs, (2 * h + 1 - core) * share + i).astype(BF16)
                return carry

            lax.fori_loop(0, share, block, 0)


def backward_kernel(
    step, unroll, src, dst, meta, tiles, first, second, own_a, send_a, own_b, send_b, panel, sem, *accs
):
    half = panel.shape[0] // 2

    @pl.when(pl.program_id(0) == 0)
    def _():
        one = pltpu.make_async_copy(first, panel.at[pl.ds(0, half)], sem.at[0])
        two = pltpu.make_async_copy(second, panel.at[pl.ds(half, half)], sem.at[1])
        one.start()
        two.start()
        one.wait()
        two.wait()

    accumulate(True, step, unroll, meta[0], src, dst, tiles, panel, accs)

    @pl.when(pl.program_id(0) == pl.num_programs(0) - 1)
    def _():
        part = own_a.shape[0]
        for own, send, base, bit in ((own_a, send_a, 0, meta[1]), (own_b, send_b, 2 * part, meta[2])):

            def block(i, carry):
                own[i] = total(accs, base + bit * part + i)
                send[i] = total(accs, base + (1 - bit) * part + i).astype(BF16)
                return carry

            lax.fori_loop(0, part, block, 0)


STEP = 64
UNROLL = 32
SUMS = 4


def tile_spec(step, tile):
    def at(g, src, dst, meta):
        return (jnp.minimum(g, jnp.maximum((meta[0] - 1) // step, 0)), 0, 0)

    return pl.BlockSpec((step, tile, tile), at)


def whole(shape):
    return pl.BlockSpec(shape, lambda g, *_: (0,) * len(shape), pipeline_mode=pl.Buffered(1))


def forward(src, dst, meta, tiles, panel, shares):
    slots, tile, _ = tiles.shape
    groups, _, width = panel.shape
    shape = (shares // 2, groups // shares, tile, width)
    return pl.pallas_call(
        functools.partial(forward_kernel, STEP, UNROLL),
        grid_spec=pltpu.PrefetchScalarGridSpec(
            num_scalar_prefetch=3,
            grid=(slots // STEP,),
            in_specs=[tile_spec(STEP, tile), whole(panel.shape)],
            out_specs=[whole(shape), whole(shape)],
            scratch_shapes=[pltpu.VMEM((groups + 1, tile, width), F32)] * SUMS,
        ),
        out_shape=[jax.ShapeDtypeStruct(shape, F32), jax.ShapeDtypeStruct(shape, BF16)],
        compiler_params=pltpu.CompilerParams(
            vmem_limit_bytes=56 * 2**20, dimension_semantics=("arbitrary",)
        ),
        name="forward",
    )(src, dst, meta, tiles, panel)


def backward(src, dst, meta, tiles, first, second, groups):
    slots, tile, _ = tiles.shape
    half, _, width = first.shape
    shape = (groups // 4, tile, width)
    outs = [jax.ShapeDtypeStruct(shape, F32), jax.ShapeDtypeStruct(shape, BF16)]
    return pl.pallas_call(
        functools.partial(backward_kernel, STEP, UNROLL),
        grid_spec=pltpu.PrefetchScalarGridSpec(
            num_scalar_prefetch=3,
            grid=(slots // STEP,),
            in_specs=[
                tile_spec(STEP, tile),
                pl.BlockSpec(memory_space=pl.ANY),
                pl.BlockSpec(memory_space=pl.ANY),
            ],
            out_specs=[whole(shape)] * 4,
            scratch_shapes=[
                pltpu.VMEM((2 * half, tile, width), BF16),
                pltpu.SemaphoreType.DMA((2,)),
            ]
            + [pltpu.VMEM((groups + 1, tile, width), F32)] * SUMS,
        ),
        out_shape=outs * 2,
        compiler_params=pltpu.CompilerParams(
            vmem_limit_bytes=56 * 2**20, dimension_semantics=("arbitrary",)
        ),
        name="backward",
    )(src, dst, meta, tiles, first, second)


def halves(x, bit):
    n = x.shape[0] // 2
    return (
        lax.dynamic_slice_in_dim(x, bit * n, n, 0),
        lax.dynamic_slice_in_dim(x, (1 - bit) * n, n, 0),
    )


def joined(own, other, bit):
    return jnp.where(bit == 0, jnp.concatenate([own, other]), jnp.concatenate([other, own]))


def reduce_rest(own, arrived, bits):
    value = own + arrived.astype(F32)
    for bit in bits[1:-1]:
        keep, give = halves(value, bit_of("img", bit))
        value = keep + swap(give.astype(BF16), "img", bit).astype(F32)
    mine = value.astype(BF16)
    return mine.astype(F32) + swap(mine, "img", bits[-1]).astype(F32)


def scatter_start(x, bits):
    for bit in bits[:-1]:
        x = halves(x, bit_of("img", bit))[0]
    return x


def gather_back(x, bits):
    for bit in reversed(bits[:-1]):
        x = joined(x, swap(x, "img", bit), bit_of("img", bit))
    return x


def body(tile_values, tile_rows, tile_cols, tile_count, row_degree, col_degree, start_panel):
    slots, tile, _ = tile_values.shape
    width = start_panel.shape[1]
    row_total = row_degree.shape[0]
    col_total = col_degree.shape[0]
    row_groups = row_total // tile
    col_groups = col_total // tile
    rows = tile_rows[0]
    cols = tile_cols[0]
    count = tile_count[0, 0]
    caps = lax.axis_size("cap")
    imgs = lax.axis_size("img")
    cap_bits = caps.bit_length() - 1
    img_bits = imgs.bit_length() - 1
    core = bit_of("cap", 0)
    root = math.sqrt(row_total * imgs)
    share = row_groups // caps
    row_scale = (1.0 / jnp.sqrt(row_degree)).reshape(caps // 2, 2, share, tile, 1)
    col_scale = (1.0 / jnp.sqrt(col_degree)).reshape(col_groups, tile, 1)
    scaled_start = (start_panel.astype(F32).reshape(col_groups, tile, width) * col_scale).astype(BF16)

    own, send = forward(cols, rows, jnp.stack([count, core]), tile_values, scaled_start, caps)
    part = own + swap(send, "cap", 0).astype(F32)
    for bit in range(1, cap_bits):
        part = part + swap(part.astype(BF16), "cap", bit).astype(F32)
    own_scale = lax.dynamic_index_in_dim(row_scale, core, 1, False)
    image = part * own_scale
    scaled = (image * own_scale).astype(BF16).reshape(row_groups // 2, tile, width)
    other = swap(scaled, "cap", 0)

    block = rows // share
    place = ((block & 1) ^ core) * (row_groups // 2) + (block >> 1) * share + rows % share
    order_a = list(range(img_bits))
    order_b = order_a[1:] + order_a[:1]
    own_a, send_a, own_b, send_b = backward(
        place,
        cols,
        jnp.stack([count, bit_of("img", order_a[0]), bit_of("img", order_b[0])]),
        tile_values,
        scaled,
        other,
        col_groups,
    )
    scale_a, scale_b = col_scale[: col_groups // 2], col_scale[col_groups // 2 :]
    got_a = swap(send_a, "img", order_a[0])
    got_b = swap(send_b, "img", order_b[0])
    sum_a = reduce_rest(own_a, got_a, order_a)
    sum_b = reduce_rest(own_b, got_b, order_b)
    next_a = (sum_a * scatter_start(scale_a, order_a)).astype(BF16)
    next_b = (sum_b * scatter_start(scale_b, order_b)).astype(BF16)
    next_panel = jnp.concatenate(
        [gather_back(next_a, order_a), gather_back(next_b, order_b)]
    ).reshape(col_total, width)

    mine = lax.dynamic_index_in_dim(image, lax.axis_index("cap") >> 1, 0, False).reshape(
        share * tile, width
    )
    gram = jnp.dot(mine.T, mine, precision=lax.Precision.HIGHEST, preferred_element_type=F32)
    for axis, bits in (("cap", cap_bits), ("img", img_bits)):
        for bit in range(bits):
            gram = gram + swap(gram, axis, bit)
    lower = jnp.linalg.cholesky(gram)
    basis = (
        lax.linalg.triangular_solve(lower, mine, left_side=False, lower=True, transpose_a=True) * root
    )
    factor = lower.T / root
    return (basis, factor, next_panel)


def solution(mesh):
    placed = (
        P("img", "cap", None),
        P("img", "cap"),
        P("img", "cap"),
        P("img", "cap"),
        P("img"),
        P("cap"),
        P("cap", None),
    )
    return jax.shard_map(
        body,
        mesh=mesh,
        in_specs=placed,
        out_specs=(P(("img", "cap"), None), P(), P("cap", None)),
        check_vma=False,
    )
```

```python
import functools
import math

import jax
import jax.numpy as jnp
from jax import lax
from jax.experimental import pallas as pl
from jax.experimental.pallas import tpu as pltpu
from jax.experimental.layout import Layout, with_layout_constraint
from jax.sharding import PartitionSpec as P

F32 = jnp.float32
BF16 = jnp.bfloat16


def row_major(x):
    return with_layout_constraint(x, Layout(major_to_minor=tuple(range(x.ndim))))


def swap(x, axis, bit):
    n = lax.axis_size(axis)
    return row_major(lax.ppermute(row_major(x), axis, [(i, i ^ (1 << bit)) for i in range(n)]))


def bit_of(axis, bit):
    return (lax.axis_index(axis) >> bit) & 1


UNROLL = 32


def iota(shape, dim):
    return lax.broadcasted_iota(jnp.int32, shape, dim)


def ones_where(mask, dtype=BF16):
    return jnp.where(mask, 1.0, 0.0).astype(dtype)


def build_list(groups, places, key, live, values):
    slots = key.shape[1]
    member = jnp.where((key == iota((groups, slots), 0)) & live, 1.0, 0.0)
    earlier = ones_where(iota((slots, slots), 0) < iota((slots, slots), 1))
    within = jnp.dot(member.astype(BF16), earlier, preferred_element_type=F32)
    size = 2.0 * jnp.floor((jnp.sum(member, axis=1, keepdims=True) + 1.0) * 0.5)
    lower = ones_where(iota((groups, groups), 1) < iota((groups, groups), 0))
    spread = jnp.broadcast_to(size, (groups, 128)).astype(BF16)
    first = jnp.dot(lower, spread, preferred_element_type=F32)[:, :1]
    place = jnp.sum(member * (within + first), axis=0, keepdims=True)
    place = jnp.where(live, place, -1.0).astype(jnp.int32)
    taken = ones_where(place == iota((places, slots), 0))
    row = iota((8, slots), 0)
    stacked = jnp.where(row == 0, 1, 0)
    for i, value in enumerate(values):
        stacked = jnp.where(row == i + 1, value, stacked)
    found = lax.dot_general(
        stacked.astype(F32).astype(BF16), taken, (((1,), (1,)), ((), ())), preferred_element_type=F32
    )
    return [found[i + 1 : i + 2] for i in range(len(values))], found[0:1], size


def pack_rows(rows, places):
    row = iota((8, places), 0)
    packed = jnp.zeros((8, places), F32)
    for i, value in enumerate(rows):
        packed = jnp.where(row == i, value, packed)
    return packed.astype(jnp.int32)


def add_pair(transposed, tiles, at, panel, places, acc, to):
    two = [tiles[at[0]], tiles[at[1]]]
    panels = jnp.concatenate([panel[places[0]], panel[places[1]]], axis=0)
    if transposed:
        dims = (((0,), (0,)), ((), ()))
        left = jnp.concatenate(two, axis=0)
    else:
        dims = (((1,), (0,)), ((), ()))
        left = jnp.concatenate(two, axis=1)
    acc[to] += lax.dot_general(left, panels, dims, preferred_element_type=F32)


def split_out(acc, base, shares, size, core, own, send):
    for h in range(shares // 2):

        def block(i, carry):
            own[h * size + i] = acc[base + (2 * h + core) * size + i]
            send[h * size + i] = acc[base + (2 * h + 1 - core) * size + i].astype(BF16)
            return carry

        lax.fori_loop(0, size, block, 0, unroll=2)


def fetch(order, first, tiles, held, sem, chunk):
    slots = sem.shape[0]
    slot = lax.rem(chunk, slots)
    for j in range(2 * UNROLL):
        tile = order[0, first + chunk * 2 * UNROLL + j]
        pltpu.make_async_copy(tiles.at[tile], held.at[slot * 2 * UNROLL + j], sem.at[slot]).start()


def multiply(transposed, order, first, pairs, dead, tiles, held, sem, panel, acc, ahead=lambda: None):
    slots = sem.shape[0]
    chunks = pl.cdiv(pairs, UNROLL)

    def begin(chunk, carry):
        fetch(order, first, tiles, held, sem, chunk)
        return carry

    lax.fori_loop(0, jnp.minimum(chunks, slots), begin, 0)
    ahead()

    def work(chunk, carry):
        slot = lax.rem(chunk, slots)
        whole = pl.ds(slot * 2 * UNROLL, 2 * UNROLL)
        pltpu.make_async_copy(tiles.at[pl.ds(0, 2 * UNROLL)], held.at[whole], sem.at[slot]).wait()
        for j in range(UNROLL):
            q = chunk * UNROLL + j
            p = first + 2 * q
            h = slot * 2 * UNROLL + 2 * j
            to = jnp.where(q < pairs, order[2, p], dead)
            add_pair(transposed, held, (h, h + 1), panel, (order[1, p], order[1, p + 1]), acc, to)

        @pl.when(chunk + slots < chunks)
        def _():
            fetch(order, first, tiles, held, sem, chunk + slots)

        return carry

    lax.fori_loop(0, chunks, work, 0)


def shares_of(row, share):
    return row >> (share.bit_length() - 1), row & (share - 1)


def order_rows(found, taken, size, blocks, groups):
    high, low, source, target = found
    return [
        high * 64.0 + low,
        source + (1.0 - taken) * blocks,
        target + (1.0 - taken) * groups,
        0.5 * jnp.sum(size, axis=0, keepdims=True),
    ]


def image_kernel(
    shares, cut, meta, rows_h, cols_h, degree_h, start, tiles,
    own_one, own_two, send,
    acc, rows, cols, degree, panel, order, order_s, held, in_sem, order_sem, tile_sem,
):
    groups = degree.shape[0]
    share = groups // shares
    slots = rows.shape[1]
    places = order.shape[1]
    copies = [
        pltpu.make_async_copy(source, target, in_sem.at[i])
        for i, (source, target) in enumerate(
            ((rows_h, rows), (cols_h, cols), (degree_h, degree), (start, panel.at[pl.ds(0, groups)]))
        )
    ]
    for copy in copies:
        copy.start()
    count, core = meta[0], meta[1]
    copies[0].wait()
    copies[1].wait()
    lane = iota((1, slots), 1)
    row, col = rows[...], cols[...]
    part, at = shares_of(row, share)
    key = jnp.where(at < cut, part * cut + at, shares * cut + part * (share - cut) + at - cut)
    found, taken, size = build_list(
        groups, places, key, lane < count, [lane >> 6, lane & 63, col, key]
    )
    order[...] = pack_rows(order_rows(found, taken, size, groups, groups), places)
    order_copy = pltpu.make_async_copy(order, order_s, order_sem)
    order_copy.start()
    acc[...] = jnp.zeros_like(acc)
    order_copy.wait()

    def ahead():
        copies[2].wait()
        copies[3].wait()
        scale = lax.transpose(lax.rsqrt(degree[...]), (1, 0))
        for g in range(groups):
            panel[g] = (panel[g].astype(F32) * scale[:, g : g + 1]).astype(BF16)
        panel[groups] = jnp.zeros(panel.shape[1:], BF16)

    multiply(False, order_s, 0, order_s[3, 0], groups, tiles, held, tile_sem, panel, acc, ahead)
    split_out(acc, 0, shares, cut, core, own_one, send.at[pl.ds(0, own_one.shape[0])])
    split_out(
        acc, shares * cut, shares, share - cut, core, own_two,
        send.at[pl.ds(own_one.shape[0], own_two.shape[0])],
    )


def order_kernel(shares, cut, groups, meta, rows, cols, back_one, back_two):
    share = groups // shares
    slots = rows.shape[1]
    places = back_one.shape[1]
    count, core = meta[0], meta[1]
    lane = iota((1, slots), 1)
    row, col = rows[...], cols[...]
    part, at = shares_of(row, share)
    for out, size, piece, inside in (
        (back_one, cut, at < cut, at),
        (back_two, share - cut, at >= cut, at - cut),
    ):
        blocks = shares * size
        place = ((part & 1) ^ core) * (blocks // 2) + (part >> 1) * size + inside
        found, taken, padded = build_list(
            groups, places, col, (lane < count) & piece, [lane >> 6, lane & 63, place, col]
        )
        out[...] = pack_rows(order_rows(found, taken, padded, blocks, groups), places)


def caption_part(order, tiles, mine, other, acc, panel, held, sem, tile_sem, fill):
    half = mine.shape[0]
    copies = [
        pltpu.make_async_copy(source, panel.at[pl.ds(i * half, half)], sem.at[i])
        for i, source in enumerate((mine, other))
    ]

    def ahead():
        for copy in copies:
            copy.start()
        panel[2 * half] = jnp.zeros(panel.shape[1:], BF16)
        fill()
        for copy in copies:
            copy.wait()

    multiply(
        True, order, 0, order[3, 0], acc.shape[0] - 1, tiles, held, tile_sem, panel, acc, ahead
    )


def third_kernel(order, tiles, mine, other, acc, mark, panel, held, sem, tile_sem):
    mark[...] = jnp.zeros_like(mark)

    def fill():
        acc[...] = jnp.zeros_like(acc)

    caption_part(order, tiles, mine, other, acc, panel, held, sem, tile_sem, fill)


def fourth_kernel(
    meta, order, tiles, before_h, mine, other, own_a, send_a, own_b, send_b,
    acc, before, panel, held, sem, before_sem, tile_sem,
):
    copy = pltpu.make_async_copy(before_h, before, before_sem)
    copy.start()

    def fill():
        acc[...] = jnp.zeros_like(acc)

    caption_part(order, tiles, mine, other, acc, panel, held, sem, tile_sem, fill)
    copy.wait()
    part = own_a.shape[0]
    for own, send, base, bit in ((own_a, send_a, 0, meta[0]), (own_b, send_b, 2 * part, meta[1])):

        def block(i, carry):
            keep, give = base + bit * part + i, base + (1 - bit) * part + i
            own[i] = acc[keep] + before[keep]
            send[i] = (acc[give] + before[give]).astype(BF16)
            return carry

        lax.fori_loop(0, part, block, 0, unroll=2)


def factor_kernel(root, gram, upper, inverse, rest, left):
    size = gram.shape[0]
    rest[...] = gram[...]
    left[...] = ones_where(iota((size, size), 0) == iota((size, size), 1), F32)
    row = iota((8, size), 0)
    for base in range(0, size, 8):
        panel = pl.ds(base, 8)
        u, m = rest[panel, :], left[panel, :]
        columns = [jnp.broadcast_to(u[:, base + k : base + k + 1], (8, size)) for k in range(8)]
        scale = jnp.zeros((8, size), F32)
        for s in range(8):
            pivot = columns[s][s : s + 1]
            scale = jnp.where(row == s, lax.rsqrt(pivot), scale)
            f = jnp.where(row > s, columns[s] / pivot, 0.0)
            for k in range(s + 1, 8):
                columns[k] = columns[k] - f * columns[k][s : s + 1]
            u = u - f * u[s : s + 1]
            m = m - f * m[s : s + 1]
        u = jnp.where(iota((8, size), 1) >= row + base, u * scale, 0.0)
        m = m * scale
        upper[panel, :] = u * (1.0 / root)
        inverse[panel, :] = m * root
        if base + 8 < size:
            both = lax.dot_general(
                u,
                jnp.concatenate([u, m], axis=1),
                (((0,), (0,)), ((), ())),
                precision=lax.Precision.HIGHEST,
                preferred_element_type=F32,
            )
            rest[...] -= both[:, :size]
            left[...] -= both[:, size:]


VMEM = pl.BlockSpec(memory_space=pltpu.VMEM)
SMEM = pl.BlockSpec(memory_space=pltpu.SMEM)
ANY = pl.BlockSpec(memory_space=pl.ANY)
HBM = pl.BlockSpec(memory_space=pltpu.HBM)
PARAMS = pltpu.CompilerParams(vmem_limit_bytes=32 * 2**20)
DEPTH = 4


def in_hbm(x):
    return pltpu.with_memory_space_constraint(x, pltpu.HBM)


def buffers(tile):
    return [
        pltpu.VMEM((DEPTH * 2 * UNROLL, tile, tile), BF16),
        pltpu.SemaphoreType.DMA((DEPTH,)),
    ]


def places_of(slots, groups):
    return (pl.cdiv(slots + groups, 2 * UNROLL) + 1) * 2 * UNROLL


def forward(shares, cut, meta, rows, cols, degree, start, tiles):
    slots, tile, _ = tiles.shape
    groups, _, width = start.shape
    places = places_of(slots, groups)
    block = (tile, width)
    one = shares // 2 * cut
    two = groups // 2 - one
    held, tile_sem = buffers(tile)
    return pl.pallas_call(
        functools.partial(image_kernel, shares, cut),
        in_specs=[SMEM] + [HBM] * 5,
        out_specs=[VMEM] * 3,
        out_shape=[
            jax.ShapeDtypeStruct((one, *block), F32),
            jax.ShapeDtypeStruct((two, *block), F32),
            jax.ShapeDtypeStruct((one + two, *block), BF16),
        ],
        scratch_shapes=[
            pltpu.VMEM((groups + 1, *block), F32),
            pltpu.VMEM((1, slots), jnp.int32),
            pltpu.VMEM((1, slots), jnp.int32),
            pltpu.VMEM((groups, tile), F32),
            pltpu.VMEM((groups + 1, *block), BF16),
            pltpu.VMEM((8, places), jnp.int32),
            pltpu.SMEM((8, places), jnp.int32),
            held,
            pltpu.SemaphoreType.DMA((4,)),
            pltpu.SemaphoreType.DMA,
            tile_sem,
        ],
        compiler_params=PARAMS,
        name="image",
    )(meta, *map(in_hbm, (rows, cols, degree, start, tiles)))


def back_orders(shares, cut, groups, meta, rows, cols):
    listing = jax.ShapeDtypeStruct((8, places_of(rows.shape[1], groups)), jnp.int32)
    return pl.pallas_call(
        functools.partial(order_kernel, shares, cut, groups),
        in_specs=[SMEM, VMEM, VMEM],
        out_specs=[VMEM] * 2,
        out_shape=[listing] * 2,
        compiler_params=PARAMS,
        name="orders",
    )(meta, rows, cols)


def backward_one(groups, order, tiles, mine, other):
    block = mine.shape[1:]
    held, tile_sem = buffers(block[0])
    return pl.pallas_call(
        third_kernel,
        in_specs=[SMEM, HBM, ANY, ANY],
        out_specs=[VMEM] * 2,
        out_shape=[
            jax.ShapeDtypeStruct((groups + 1, *block), F32),
            jax.ShapeDtypeStruct((1, 128), F32),
        ],
        scratch_shapes=[
            pltpu.VMEM((2 * mine.shape[0] + 1, *block), BF16),
            held,
            pltpu.SemaphoreType.DMA((2,)),
            tile_sem,
        ],
        compiler_params=PARAMS,
        name="caption_one",
    )(order, in_hbm(tiles), mine, other)


def backward_two(groups, meta, order, tiles, before, mine, other):
    block = mine.shape[1:]
    part = groups // 4
    held, tile_sem = buffers(block[0])
    total = pltpu.VMEM((groups + 1, *block), F32)
    return pl.pallas_call(
        fourth_kernel,
        in_specs=[SMEM, SMEM, HBM, HBM, ANY, ANY],
        out_specs=[VMEM] * 4,
        out_shape=[
            jax.ShapeDtypeStruct((part, *block), F32),
            jax.ShapeDtypeStruct((part, *block), BF16),
        ]
        * 2,
        scratch_shapes=[
            total,
            total,
            pltpu.VMEM((2 * mine.shape[0] + 1, *block), BF16),
            held,
            pltpu.SemaphoreType.DMA((2,)),
            pltpu.SemaphoreType.DMA,
            tile_sem,
        ],
        compiler_params=PARAMS,
        name="caption_two",
    )(meta, order, in_hbm(tiles), in_hbm(before), mine, other)


def factorize(gram, root):
    shape = jax.ShapeDtypeStruct(gram.shape, F32)
    return pl.pallas_call(
        functools.partial(factor_kernel, root),
        in_specs=[VMEM],
        out_specs=[VMEM] * 2,
        out_shape=[shape] * 2,
        scratch_shapes=[pltpu.VMEM(gram.shape, F32)] * 2,
        name="factorize",
    )(gram)


def halves(x, bit):
    n = x.shape[0] // 2
    return (
        lax.dynamic_slice_in_dim(x, bit * n, n, 0),
        lax.dynamic_slice_in_dim(x, (1 - bit) * n, n, 0),
    )


def joined(own, other, bit):
    return jnp.where(bit == 0, jnp.concatenate([own, other]), jnp.concatenate([other, own]))


def rounded(x):
    return lax.reduce_precision(x, exponent_bits=8, mantissa_bits=7).astype(BF16)


def in_two(x):
    high = rounded(x)
    return jnp.stack([high, rounded(x - high.astype(F32))])


def from_two(x):
    return x[0].astype(F32) + x[1].astype(F32)


def swap_with(x, extra, axis, bit):
    size = x.shape[0]
    arrived = swap(jnp.concatenate([x, extra]), axis, bit)
    return arrived[:size], in_two(from_two(extra) + from_two(arrived[size:]))


def reduce_rest(own, arrived, bits, extra=None):
    parts = [own, arrived]
    for i, bit in enumerate(bits[1:]):
        last = i == len(bits) - 2
        if last:
            give = rounded(sum(x.astype(F32) for x in parts))
            parts = [give]
        else:
            split = [halves(x, bit_of("img", bit)) for x in parts]
            give = rounded(sum(x.astype(F32) for _, x in split))
            parts = [x for x, _ in split]
        if extra is None:
            arrived = swap(give, "img", bit)
        else:
            arrived, extra = swap_with(give, extra, "img", bit)
        parts.append(arrived)
    return sum(x.astype(F32) for x in parts), extra


def scatter_start(x, bits):
    for bit in bits[:-1]:
        x = halves(x, bit_of("img", bit))[0]
    return x


def gather_back(x, bits, extra=None, along=None):
    for bit in reversed(bits[:-1]):
        if bit == along:
            arrived, extra = swap_with(x, extra, "img", bit)
        else:
            arrived = swap(x, "img", bit)
        x = joined(x, arrived, bit_of("img", bit))
    return x, extra


def body(tile_values, tile_rows, tile_cols, tile_count, row_degree, col_degree, start_panel):
    slots, tile, _ = tile_values.shape
    width = start_panel.shape[1]
    row_total = row_degree.shape[0]
    col_total = col_degree.shape[0]
    row_groups = row_total // tile
    col_groups = col_total // tile
    caps = lax.axis_size("cap")
    imgs = lax.axis_size("img")
    cap_bits = caps.bit_length() - 1
    img_bits = imgs.bit_length() - 1
    core = bit_of("cap", 0)
    chip = lax.axis_index("cap") >> 1
    root = math.sqrt(row_total * imgs)
    share = row_groups // caps
    cut = share // 2
    count = tile_count[0, 0]
    row_scale = (1.0 / jnp.sqrt(row_degree)).reshape(caps // 2, 2, share, tile, 1)
    row_scale = lax.dynamic_index_in_dim(row_scale, core, 1, False)
    col_scale = (1.0 / jnp.sqrt(col_degree)).reshape(col_groups, tile, 1)
    degree = col_degree.reshape(col_groups, tile)
    start = start_panel.reshape(col_groups, tile, width)

    meta = jnp.stack([count, core])
    own_one, own_two, send = forward(
        caps, cut, meta, tile_rows, tile_cols, degree, start, tile_values
    )
    came = swap(send, "cap", 0)
    size = own_one.shape[0]
    first = rounded(own_one + came[:size].astype(F32))
    second = rounded(own_two + came[size:].astype(F32))
    order_one, order_two = back_orders(caps, cut, col_groups, meta, tile_rows, tile_cols)

    def over_chips(part):
        part = part.astype(F32)
        for bit in range(1, cap_bits):
            part = rounded(part)
            part = part.astype(F32) + swap(part, "cap", bit).astype(F32)
        return part

    def finish(part, scale):
        scale = scale.reshape(-1, tile, 1)
        image = part * scale
        mine = (image * scale).astype(BF16)
        return image, mine, swap(mine, "cap", 0)

    def products(image):
        flat = image.reshape(-1, width)
        return jnp.dot(flat.T, flat, precision=lax.Precision.HIGHEST, preferred_element_type=F32)

    scale_one, scale_two = row_scale[:, :cut], row_scale[:, cut:]
    order_one, scale_one = lax.optimization_barrier((order_one, scale_one))
    first, second = over_chips(first), over_chips(second)
    image_one, mine, other = finish(first, scale_one)
    gram = products(image_one)
    before, mark = backward_one(col_groups, order_one, tile_values, mine, other)
    gram, scale_two = lax.optimization_barrier((gram, scale_two + mark[0, 0]))
    image_two, mine, other = finish(second, scale_two)

    order_a = list(range(img_bits))
    order_b = [1, 0, *range(2, img_bits)]
    own_a, send_a, own_b, send_b = backward_two(
        col_groups,
        jnp.stack([bit_of("img", order_a[0]), bit_of("img", order_b[0])]),
        order_two,
        tile_values,
        before,
        mine,
        other,
    )
    send_a, send_b, image_two = lax.optimization_barrier((send_a, send_b, image_two))
    scale_a, scale_b = col_scale[: col_groups // 2], col_scale[col_groups // 2 :]
    got_a = swap(send_a, "img", order_a[0])
    got_b = swap(send_b, "img", order_b[0])
    gram = gram + products(image_two)
    gram = in_two(gram + swap(gram, "cap", 0))
    sum_a, gram = reduce_rest(own_a, got_a, order_a, gram)
    sum_b, _ = reduce_rest(own_b, got_b, order_b)
    next_a = (sum_a * scatter_start(scale_a, order_a)).astype(BF16)
    next_b = (sum_b * scatter_start(scale_b, order_b)).astype(BF16)
    next_b, gram = gather_back(next_b, order_b, gram, order_a[0])
    next_a, _ = gather_back(next_a, order_a)
    next_panel = jnp.concatenate([next_a, next_b]).reshape(col_total, width)

    factor, inverse = factorize(from_two(gram), root)
    rows = jnp.concatenate(
        [
            lax.dynamic_index_in_dim(image.reshape(caps // 2, -1, tile, width), chip, 0, False)
            for image in (image_one, image_two)
        ]
    ).reshape(share * tile, width)
    basis = lax.dot_general(
        rows,
        inverse,
        (((1,), (1,)), ((), ())),
        precision=lax.Precision.HIGHEST,
        preferred_element_type=F32,
    )
    return (basis, factor, next_panel)


def solution(mesh):
    placed = (
        P("img", "cap", None),
        P("img", "cap"),
        P("img", "cap"),
        P("img", "cap"),
        P("img"),
        P("cap"),
        P("cap", None),
    )
    return jax.shard_map(
        body,
        mesh=mesh,
        in_specs=placed,
        out_specs=(P(("img", "cap"), None), P(), P("cap", None)),
        check_vma=False,
    )
```

```python
import functools
import math

import jax
import jax.numpy as jnp
from jax import lax
from jax.experimental import pallas as pl
from jax.experimental.pallas import tpu as pltpu
from jax.experimental.layout import Layout, with_layout_constraint
from jax.sharding import PartitionSpec as P

F32 = jnp.float32
BF16 = jnp.bfloat16


def row_major(x):
    return with_layout_constraint(x, Layout(major_to_minor=tuple(range(x.ndim))))


def swap(x, axis, bit):
    n = lax.axis_size(axis)
    return row_major(lax.ppermute(row_major(x), axis, [(i, i ^ (1 << bit)) for i in range(n)]))


def bit_of(axis, bit):
    return (lax.axis_index(axis) >> bit) & 1


UNROLL = 32


def iota(shape, dim):
    return lax.broadcasted_iota(jnp.int32, shape, dim)


def ones_where(mask, dtype=BF16):
    return jnp.where(mask, 1.0, 0.0).astype(dtype)


def build_list(groups, places, key, live, values):
    slots = key.shape[1]
    member = jnp.where((key == iota((groups, slots), 0)) & live, 1.0, 0.0)
    earlier = ones_where(iota((slots, slots), 0) < iota((slots, slots), 1))
    within = jnp.dot(member.astype(BF16), earlier, preferred_element_type=F32)
    size = 2.0 * jnp.floor((jnp.sum(member, axis=1, keepdims=True) + 1.0) * 0.5)
    lower = ones_where(iota((groups, groups), 1) < iota((groups, groups), 0))
    spread = jnp.broadcast_to(size, (groups, 128)).astype(BF16)
    first = jnp.dot(lower, spread, preferred_element_type=F32)[:, :1]
    place = jnp.sum(member * (within + first), axis=0, keepdims=True)
    place = jnp.where(live, place, -1.0).astype(jnp.int32)
    taken = ones_where(place == iota((places, slots), 0))
    row = iota((8, slots), 0)
    stacked = jnp.where(row == 0, 1, 0)
    for i, value in enumerate(values):
        stacked = jnp.where(row == i + 1, value, stacked)
    found = lax.dot_general(
        stacked.astype(F32).astype(BF16), taken, (((1,), (1,)), ((), ())), preferred_element_type=F32
    )
    return [found[i + 1 : i + 2] for i in range(len(values))], found[0:1], size


def pack_rows(rows, places):
    row = iota((8, places), 0)
    packed = jnp.zeros((8, places), F32)
    for i, value in enumerate(rows):
        packed = jnp.where(row == i, value, packed)
    return packed.astype(jnp.int32)


def add_pair(transposed, tiles, at, panel, places, acc, to):
    two = [tiles[at[0]], tiles[at[1]]]
    panels = jnp.concatenate([panel[places[0]], panel[places[1]]], axis=0)
    if transposed:
        dims = (((0,), (0,)), ((), ()))
        left = jnp.concatenate(two, axis=0)
    else:
        dims = (((1,), (0,)), ((), ()))
        left = jnp.concatenate(two, axis=1)
    acc[to] += lax.dot_general(left, panels, dims, preferred_element_type=F32)


def split_out(acc, base, shares, size, core, own, send):
    for h in range(shares // 2):

        def block(i, carry):
            own[h * size + i] = acc[base + (2 * h + core) * size + i]
            send[h * size + i] = acc[base + (2 * h + 1 - core) * size + i].astype(BF16)
            return carry

        lax.fori_loop(0, size, block, 0, unroll=2)


def fetch_one(order, tiles, held, sem, chunk, j):
    slot = lax.rem(chunk, sem.shape[0])
    tile = order[0, chunk * 2 * UNROLL + j]
    pltpu.make_async_copy(tiles.at[tile], held.at[slot * 2 * UNROLL + j], sem.at[slot]).start()


def multiply(transposed, order, pairs, dead, tiles, held, sem, panel, acc, meanwhile):
    slots = sem.shape[0]
    ahead = slots - 1
    chunks = jnp.maximum(pl.cdiv(pairs, UNROLL), ahead)
    starts = ahead * 2 * UNROLL
    done = 0
    for i in range(starts):
        fetch_one(order, tiles, held, sem, i // (2 * UNROLL), i % (2 * UNROLL))
        while done * starts < (i + 1) * len(meanwhile):
            meanwhile[done]()
            done += 1

    def work(more, chunk, carry):
        slot = lax.rem(chunk, slots)
        whole = pl.ds(slot * 2 * UNROLL, 2 * UNROLL)
        pltpu.make_async_copy(tiles.at[pl.ds(0, 2 * UNROLL)], held.at[whole], sem.at[slot]).wait()
        for j in range(UNROLL):
            if more:
                for k in (2 * j, 2 * j + 1):
                    fetch_one(order, tiles, held, sem, chunk + ahead, k)
            q = chunk * UNROLL + j
            p = 2 * q
            h = slot * 2 * UNROLL + 2 * j
            to = jnp.where(q < pairs, order[2, p], dead)
            add_pair(transposed, held, (h, h + 1), panel, (order[1, p], order[1, p + 1]), acc, to)
        return carry

    steady = chunks - ahead
    lax.fori_loop(0, steady, functools.partial(work, True), 0)
    lax.fori_loop(steady, chunks, functools.partial(work, False), 0)


def shares_of(row, share):
    return row >> (share.bit_length() - 1), row & (share - 1)


def order_rows(found, taken, size, blocks, groups):
    high, low, source, target = found
    return [
        high * 64.0 + low,
        source + (1.0 - taken) * blocks,
        target + (1.0 - taken) * groups,
        0.5 * jnp.sum(size, axis=0, keepdims=True),
    ]


def image_kernel(
    shares, cut, meta, rows_h, cols_h, degree_h, start, tiles,
    own_one, own_two, send,
    acc, rows, cols, degree, panel, order, order_s, held, in_sem, order_sem, tile_sem,
):
    groups = degree.shape[0]
    share = groups // shares
    slots = rows.shape[1]
    places = order.shape[1]
    copies = [
        pltpu.make_async_copy(source, target, in_sem.at[i])
        for i, (source, target) in enumerate(
            ((rows_h, rows), (cols_h, cols), (degree_h, degree), (start, panel.at[pl.ds(0, groups)]))
        )
    ]
    for copy in copies:
        copy.start()
    count, core = meta[0], meta[1]
    copies[0].wait()
    copies[1].wait()
    lane = iota((1, slots), 1)
    row, col = rows[...], cols[...]
    part, at = shares_of(row, share)
    key = jnp.where(at < cut, part * cut + at, shares * cut + part * (share - cut) + at - cut)
    found, taken, size = build_list(
        groups, places, key, lane < count, [lane >> 6, lane & 63, col, key]
    )
    order[...] = pack_rows(order_rows(found, taken, size, groups, groups), places)
    order_copy = pltpu.make_async_copy(order, order_s, order_sem)
    order_copy.start()
    acc[...] = jnp.zeros_like(acc)
    order_copy.wait()

    copies[2].wait()
    copies[3].wait()
    scale = lax.transpose(lax.rsqrt(degree[...]), (1, 0))

    def scale_block(g):
        panel[g] = (panel[g].astype(F32) * scale[:, g : g + 1]).astype(BF16)

    panel[groups] = jnp.zeros(panel.shape[1:], BF16)
    steps = [functools.partial(scale_block, g) for g in range(groups)]
    multiply(False, order_s, order_s[3, 0], groups, tiles, held, tile_sem, panel, acc, steps)
    split_out(acc, 0, shares, cut, core, own_one, send.at[pl.ds(0, own_one.shape[0])])
    split_out(
        acc, shares * cut, shares, share - cut, core, own_two,
        send.at[pl.ds(own_one.shape[0], own_two.shape[0])],
    )


def order_kernel(shares, cut, groups, meta, rows, cols, back_one, back_two):
    share = groups // shares
    slots = rows.shape[1]
    places = back_one.shape[1]
    count, core = meta[0], meta[1]
    lane = iota((1, slots), 1)
    row, col = rows[...], cols[...]
    part, at = shares_of(row, share)
    for out, size, piece, inside in (
        (back_one, cut, at < cut, at),
        (back_two, share - cut, at >= cut, at - cut),
    ):
        blocks = shares * size
        place = ((part & 1) ^ core) * (blocks // 2) + (part >> 1) * size + inside
        found, taken, padded = build_list(
            groups, places, col, (lane < count) & piece, [lane >> 6, lane & 63, place, col]
        )
        out[...] = pack_rows(order_rows(found, taken, padded, blocks, groups), places)


def caption_part(order, tiles, mine, other, acc, panel, held, sem, tile_sem):
    half = mine.shape[0]
    copies = [
        pltpu.make_async_copy(source, panel.at[pl.ds(i * half, half)], sem.at[i])
        for i, source in enumerate((mine, other))
    ]
    for copy in copies:
        copy.start()
    panel[2 * half] = jnp.zeros(panel.shape[1:], BF16)

    def clear(g):
        acc[g] = jnp.zeros(acc.shape[1:], F32)

    steps = [functools.partial(clear, g) for g in range(acc.shape[0])]
    steps += [copy.wait for copy in copies]
    dead = acc.shape[0] - 1
    multiply(True, order, order[3, 0], dead, tiles, held, tile_sem, panel, acc, steps)


def third_kernel(order, tiles, mine, other, out, mark, acc, panel, held, sem, tile_sem):
    mark[...] = jnp.zeros_like(mark)
    caption_part(order, tiles, mine, other, acc, panel, held, sem, tile_sem)

    def block(i, carry):
        out[i] = acc[i].astype(BF16)
        return carry

    lax.fori_loop(0, out.shape[0], block, 0, unroll=4)


def fourth_kernel(
    meta, order, tiles, before, mine, other, own_a, send_a, own_b, send_b,
    acc, panel, held, sem, tile_sem,
):
    caption_part(order, tiles, mine, other, acc, panel, held, sem, tile_sem)
    part = own_a.shape[0]
    for own, send, base, bit in ((own_a, send_a, 0, meta[0]), (own_b, send_b, 2 * part, meta[1])):

        def block(i, carry):
            keep, give = base + bit * part + i, base + (1 - bit) * part + i
            own[i] = acc[keep] + before[keep].astype(F32)
            send[i] = (acc[give] + before[give].astype(F32)).astype(BF16)
            return carry

        lax.fori_loop(0, part, block, 0, unroll=4)


def factor_kernel(root, gram, upper, inverse, rest, left):
    size = gram.shape[0]
    rest[...] = gram[...]
    left[...] = ones_where(iota((size, size), 0) == iota((size, size), 1), F32)
    row = iota((8, size), 0)
    for base in range(0, size, 8):
        panel = pl.ds(base, 8)
        u, m = rest[panel, :], left[panel, :]
        columns = [jnp.broadcast_to(u[:, base + k : base + k + 1], (8, size)) for k in range(8)]
        scale = jnp.zeros((8, size), F32)
        for s in range(8):
            pivot = columns[s][s : s + 1]
            root_of = lax.rsqrt(pivot)
            scale = jnp.where(row == s, root_of, scale)
            f = jnp.where(row > s, columns[s] * (root_of * root_of), 0.0)
            for k in range(s + 1, 8):
                columns[k] = columns[k] - f * columns[k][s : s + 1]
            u = u - f * u[s : s + 1]
            m = m - f * m[s : s + 1]
        u = jnp.where(iota((8, size), 1) >= row + base, u * scale, 0.0)
        m = m * scale
        upper[panel, :] = u * (1.0 / root)
        inverse[panel, :] = m * root
        if base + 8 < size:
            both = lax.dot_general(
                u,
                jnp.concatenate([u, m], axis=1),
                (((0,), (0,)), ((), ())),
                precision=lax.Precision.HIGHEST,
                preferred_element_type=F32,
            )
            rest[...] -= both[:, :size]
            left[...] -= both[:, size:]


VMEM = pl.BlockSpec(memory_space=pltpu.VMEM)
SMEM = pl.BlockSpec(memory_space=pltpu.SMEM)
ANY = pl.BlockSpec(memory_space=pl.ANY)
HBM = pl.BlockSpec(memory_space=pltpu.HBM)
PARAMS = pltpu.CompilerParams(vmem_limit_bytes=32 * 2**20)
DEPTH = 3


def in_hbm(x):
    return pltpu.with_memory_space_constraint(x, pltpu.HBM)


def buffers(tile):
    return [
        pltpu.VMEM((DEPTH * 2 * UNROLL, tile, tile), BF16),
        pltpu.SemaphoreType.DMA((DEPTH,)),
    ]


def places_of(slots, groups):
    return (pl.cdiv(slots + groups, 2 * UNROLL) + 1) * 2 * UNROLL


def forward(shares, cut, meta, rows, cols, degree, start, tiles):
    slots, tile, _ = tiles.shape
    groups, _, width = start.shape
    places = places_of(slots, groups)
    block = (tile, width)
    one = shares // 2 * cut
    two = groups // 2 - one
    held, tile_sem = buffers(tile)
    return pl.pallas_call(
        functools.partial(image_kernel, shares, cut),
        in_specs=[SMEM] + [HBM] * 5,
        out_specs=[VMEM] * 3,
        out_shape=[
            jax.ShapeDtypeStruct((one, *block), F32),
            jax.ShapeDtypeStruct((two, *block), F32),
            jax.ShapeDtypeStruct((one + two, *block), BF16),
        ],
        scratch_shapes=[
            pltpu.VMEM((groups + 1, *block), F32),
            pltpu.VMEM((1, slots), jnp.int32),
            pltpu.VMEM((1, slots), jnp.int32),
            pltpu.VMEM((groups, tile), F32),
            pltpu.VMEM((groups + 1, *block), BF16),
            pltpu.VMEM((8, places), jnp.int32),
            pltpu.SMEM((8, places), jnp.int32),
            held,
            pltpu.SemaphoreType.DMA((4,)),
            pltpu.SemaphoreType.DMA,
            tile_sem,
        ],
        compiler_params=PARAMS,
        name="image",
    )(meta, *map(in_hbm, (rows, cols, degree, start, tiles)))


def back_orders(shares, cut, groups, meta, rows, cols):
    listing = jax.ShapeDtypeStruct((8, places_of(rows.shape[1], groups)), jnp.int32)
    return pl.pallas_call(
        functools.partial(order_kernel, shares, cut, groups),
        in_specs=[SMEM, VMEM, VMEM],
        out_specs=[VMEM] * 2,
        out_shape=[listing] * 2,
        compiler_params=PARAMS,
        name="orders",
    )(meta, rows, cols)


def backward_one(groups, order, tiles, mine, other):
    block = mine.shape[1:]
    held, tile_sem = buffers(block[0])
    return pl.pallas_call(
        third_kernel,
        in_specs=[SMEM, HBM, ANY, ANY],
        out_specs=[VMEM] * 2,
        out_shape=[
            jax.ShapeDtypeStruct((groups, *block), BF16),
            jax.ShapeDtypeStruct((1, 128), F32),
        ],
        scratch_shapes=[
            pltpu.VMEM((groups + 1, *block), F32),
            pltpu.VMEM((2 * mine.shape[0] + 1, *block), BF16),
            held,
            pltpu.SemaphoreType.DMA((2,)),
            tile_sem,
        ],
        compiler_params=PARAMS,
        name="caption_one",
    )(order, in_hbm(tiles), mine, other)


def backward_two(groups, meta, order, tiles, before, mine, other):
    block = mine.shape[1:]
    part = groups // 4
    held, tile_sem = buffers(block[0])
    return pl.pallas_call(
        fourth_kernel,
        in_specs=[SMEM, SMEM, HBM, VMEM, ANY, ANY],
        out_specs=[VMEM] * 4,
        out_shape=[
            jax.ShapeDtypeStruct((part, *block), F32),
            jax.ShapeDtypeStruct((part, *block), BF16),
        ]
        * 2,
        scratch_shapes=[
            pltpu.VMEM((groups + 1, *block), F32),
            pltpu.VMEM((2 * mine.shape[0] + 1, *block), BF16),
            held,
            pltpu.SemaphoreType.DMA((2,)),
            tile_sem,
        ],
        compiler_params=PARAMS,
        name="caption_two",
    )(meta, order, in_hbm(tiles), before, mine, other)


def factorize(gram, root):
    shape = jax.ShapeDtypeStruct(gram.shape, F32)
    return pl.pallas_call(
        functools.partial(factor_kernel, root),
        in_specs=[VMEM],
        out_specs=[VMEM] * 2,
        out_shape=[shape] * 2,
        scratch_shapes=[pltpu.VMEM(gram.shape, F32)] * 2,
        name="factorize",
    )(gram)


def halves(x, bit):
    n = x.shape[0] // 2
    return (
        lax.dynamic_slice_in_dim(x, bit * n, n, 0),
        lax.dynamic_slice_in_dim(x, (1 - bit) * n, n, 0),
    )


def joined(own, other, bit):
    return jnp.where(bit == 0, jnp.concatenate([own, other]), jnp.concatenate([other, own]))


def rounded(x):
    return lax.reduce_precision(x, exponent_bits=8, mantissa_bits=7).astype(BF16)


def in_two(x):
    high = rounded(x)
    return jnp.stack([high, rounded(x - high.astype(F32))])


def from_two(x):
    return x[0].astype(F32) + x[1].astype(F32)


def swap_with(x, extra, axis, bit):
    size = x.shape[0]
    arrived = swap(jnp.concatenate([x, extra]), axis, bit)
    return arrived[:size], in_two(from_two(extra) + from_two(arrived[size:]))


def reduce_rest(own, arrived, bits, extra=None):
    parts = [own, arrived]
    for i, bit in enumerate(bits[1:]):
        last = i == len(bits) - 2
        if last:
            give = rounded(sum(x.astype(F32) for x in parts))
            parts = [give]
        else:
            split = [halves(x, bit_of("img", bit)) for x in parts]
            give = rounded(sum(x.astype(F32) for _, x in split))
            parts = [x for x, _ in split]
        if extra is None:
            arrived = swap(give, "img", bit)
        else:
            arrived, extra = swap_with(give, extra, "img", bit)
        parts.append(arrived)
    return sum(x.astype(F32) for x in parts), extra


def scatter_start(x, bits):
    for bit in bits[:-1]:
        x = halves(x, bit_of("img", bit))[0]
    return x


def gather_back(x, bits, extra=None, along=None):
    for bit in reversed(bits[:-1]):
        if bit == along:
            arrived, extra = swap_with(x, extra, "img", bit)
        else:
            arrived = swap(x, "img", bit)
        x = joined(x, arrived, bit_of("img", bit))
    return x, extra


def body(tile_values, tile_rows, tile_cols, tile_count, row_degree, col_degree, start_panel):
    slots, tile, _ = tile_values.shape
    width = start_panel.shape[1]
    row_total = row_degree.shape[0]
    col_total = col_degree.shape[0]
    row_groups = row_total // tile
    col_groups = col_total // tile
    caps = lax.axis_size("cap")
    imgs = lax.axis_size("img")
    cap_bits = caps.bit_length() - 1
    img_bits = imgs.bit_length() - 1
    core = bit_of("cap", 0)
    chip = lax.axis_index("cap") >> 1
    root = math.sqrt(row_total * imgs)
    share = row_groups // caps
    cut = share // 2
    count = tile_count[0, 0]
    row_scale = (1.0 / jnp.sqrt(row_degree)).reshape(caps // 2, 2, share, tile, 1)
    row_scale = lax.dynamic_index_in_dim(row_scale, core, 1, False)
    col_scale = (1.0 / jnp.sqrt(col_degree)).reshape(col_groups, tile, 1)
    degree = col_degree.reshape(col_groups, tile)
    start = start_panel.reshape(col_groups, tile, width)

    meta = jnp.stack([count, core])
    own_one, own_two, send = forward(
        caps, cut, meta, tile_rows, tile_cols, degree, start, tile_values
    )
    came = swap(send, "cap", 0)
    size = own_one.shape[0]
    first = rounded(own_one + came[:size].astype(F32))
    second = rounded(own_two + came[size:].astype(F32))
    order_one, order_two = back_orders(caps, cut, col_groups, meta, tile_rows, tile_cols)

    def over_chips(part):
        part = part.astype(F32)
        for bit in range(1, cap_bits):
            part = rounded(part)
            part = part.astype(F32) + swap(part, "cap", bit).astype(F32)
        return part

    def finish(part, scale):
        scale = scale.reshape(-1, tile, 1)
        image = part * scale
        mine = (image * scale).astype(BF16)
        return image, mine, swap(mine, "cap", 0)

    def products(image):
        flat = image.reshape(-1, width)
        return jnp.dot(flat.T, flat, precision=lax.Precision.HIGH, preferred_element_type=F32)

    scale_one, scale_two = row_scale[:, :cut], row_scale[:, cut:]
    order_one, scale_one = lax.optimization_barrier((order_one, scale_one))
    first, second = over_chips(first), over_chips(second)
    image_one, mine, other = finish(first, scale_one)
    gram = products(image_one)
    before, mark = backward_one(col_groups, order_one, tile_values, mine, other)
    gram, scale_two = lax.optimization_barrier((gram, scale_two + mark[0, 0]))
    image_two, mine, other = finish(second, scale_two)

    order_a = list(range(img_bits))
    order_b = [1, 0, *range(2, img_bits)]
    own_a, send_a, own_b, send_b = backward_two(
        col_groups,
        jnp.stack([bit_of("img", order_a[0]), bit_of("img", order_b[0])]),
        order_two,
        tile_values,
        before,
        mine,
        other,
    )
    send_a, send_b, image_two = lax.optimization_barrier((send_a, send_b, image_two))
    scale_a, scale_b = col_scale[: col_groups // 2], col_scale[col_groups // 2 :]
    got_a = swap(send_a, "img", order_a[0])
    got_b = swap(send_b, "img", order_b[0])
    gram = gram + products(image_two)
    gram = in_two(gram + swap(gram, "cap", 0))
    sum_a, gram = reduce_rest(own_a, got_a, order_a, gram)
    sum_b, _ = reduce_rest(own_b, got_b, order_b)
    next_a = (sum_a * scatter_start(scale_a, order_a)).astype(BF16)
    next_b = (sum_b * scatter_start(scale_b, order_b)).astype(BF16)
    next_b, gram = gather_back(next_b, order_b, gram, order_a[0])
    next_a, _ = gather_back(next_a, order_a)
    next_panel = jnp.concatenate([next_a, next_b]).reshape(col_total, width)

    factor, inverse = factorize(from_two(gram), root)
    rows = jnp.concatenate(
        [
            lax.dynamic_index_in_dim(image.reshape(caps // 2, -1, tile, width), chip, 0, False)
            for image in (image_one, image_two)
        ]
    ).reshape(share * tile, width)
    basis = lax.dot_general(
        rows,
        inverse,
        (((1,), (1,)), ((), ())),
        precision=lax.Precision.HIGH,
        preferred_element_type=F32,
    )
    return (basis, factor, next_panel)


def solution(mesh):
    placed = (
        P("img", "cap", None),
        P("img", "cap"),
        P("img", "cap"),
        P("img", "cap"),
        P("img"),
        P("cap"),
        P("cap", None),
    )
    return jax.shard_map(
        body,
        mesh=mesh,
        in_specs=placed,
        out_specs=(P(("img", "cap"), None), P(), P("cap", None)),
        check_vma=False,
    )
```

```python
import functools
import math

import jax
import jax.numpy as jnp
from jax import lax
from jax.experimental import pallas as pl
from jax.experimental.pallas import tpu as pltpu
from jax.experimental.layout import Layout, with_layout_constraint
from jax.sharding import PartitionSpec as P

F32 = jnp.float32
BF16 = jnp.bfloat16


def row_major(x):
    return with_layout_constraint(x, Layout(major_to_minor=tuple(range(x.ndim))))


def swap(x, axis, bit):
    n = lax.axis_size(axis)
    return row_major(lax.ppermute(row_major(x), axis, [(i, i ^ (1 << bit)) for i in range(n)]))


def bit_of(axis, bit):
    return (lax.axis_index(axis) >> bit) & 1


UNROLL = 32


def iota(shape, dim):
    return lax.broadcasted_iota(jnp.int32, shape, dim)


def ones_where(mask, dtype=BF16):
    return jnp.where(mask, 1.0, 0.0).astype(dtype)


def build_list(groups, places, key, live, values):
    slots = key.shape[1]
    member = jnp.where((key == iota((groups, slots), 0)) & live, 1.0, 0.0)
    earlier = ones_where(iota((slots, slots), 0) < iota((slots, slots), 1))
    within = jnp.dot(member.astype(BF16), earlier, preferred_element_type=F32)
    size = 2.0 * jnp.floor((jnp.sum(member, axis=1, keepdims=True) + 1.0) * 0.5)
    lower = ones_where(iota((groups, groups), 1) < iota((groups, groups), 0))
    spread = jnp.broadcast_to(size, (groups, 128)).astype(BF16)
    first = jnp.dot(lower, spread, preferred_element_type=F32)[:, :1]
    place = jnp.sum(member * (within + first), axis=0, keepdims=True)
    place = jnp.where(live, place, -1.0).astype(jnp.int32)
    taken = ones_where(place == iota((places, slots), 0))
    row = iota((8, slots), 0)
    stacked = jnp.where(row == 0, 1, 0)
    for i, value in enumerate(values):
        stacked = jnp.where(row == i + 1, value, stacked)
    found = lax.dot_general(
        stacked.astype(F32).astype(BF16), taken, (((1,), (1,)), ((), ())), preferred_element_type=F32
    )
    return [found[i + 1 : i + 2] for i in range(len(values))], found[0:1], size


def pack_rows(rows, places):
    row = iota((8, places), 0)
    packed = jnp.zeros((8, places), F32)
    for i, value in enumerate(rows):
        packed = jnp.where(row == i, value, packed)
    return packed.astype(jnp.int32)


def add_pair(transposed, tiles, at, panel, places, acc, to):
    two = [tiles[at[0]], tiles[at[1]]]
    panels = jnp.concatenate([panel[places[0]], panel[places[1]]], axis=0)
    if transposed:
        dims = (((0,), (0,)), ((), ()))
        left = jnp.concatenate(two, axis=0)
    else:
        dims = (((1,), (0,)), ((), ()))
        left = jnp.concatenate(two, axis=1)
    acc[to] += lax.dot_general(left, panels, dims, preferred_element_type=F32)


def split_out(acc, base, shares, size, core, own, send):
    for h in range(shares // 2):

        def block(i, carry):
            own[h * size + i] = acc[base + (2 * h + core) * size + i]
            send[h * size + i] = acc[base + (2 * h + 1 - core) * size + i].astype(BF16)
            return carry

        lax.fori_loop(0, size, block, 0, unroll=2)


def fetch_one(order, tiles, held, sem, chunk, j):
    slot = lax.rem(chunk, sem.shape[0])
    tile = order[0, chunk * 2 * UNROLL + j]
    pltpu.make_async_copy(tiles.at[tile], held.at[slot * 2 * UNROLL + j], sem.at[slot]).start()


def multiply(transposed, order, pairs, dead, tiles, held, sem, panel, acc, meanwhile):
    slots = sem.shape[0]
    ahead = slots - 1
    chunks = jnp.maximum(pl.cdiv(pairs, UNROLL), ahead)
    starts = ahead * 2 * UNROLL
    done = 0
    for i in range(starts):
        fetch_one(order, tiles, held, sem, i // (2 * UNROLL), i % (2 * UNROLL))
        while done * starts < (i + 1) * len(meanwhile):
            meanwhile[done]()
            done += 1

    def work(more, chunk, carry):
        slot = lax.rem(chunk, slots)
        whole = pl.ds(slot * 2 * UNROLL, 2 * UNROLL)
        pltpu.make_async_copy(tiles.at[pl.ds(0, 2 * UNROLL)], held.at[whole], sem.at[slot]).wait()
        for j in range(UNROLL):
            if more:
                for k in (2 * j, 2 * j + 1):
                    fetch_one(order, tiles, held, sem, chunk + ahead, k)
            q = chunk * UNROLL + j
            p = 2 * q
            h = slot * 2 * UNROLL + 2 * j
            to = jnp.where(q < pairs, order[2, p], dead)
            add_pair(transposed, held, (h, h + 1), panel, (order[1, p], order[1, p + 1]), acc, to)
        return carry

    steady = chunks - ahead
    lax.fori_loop(0, steady, functools.partial(work, True), 0)
    lax.fori_loop(steady, chunks, functools.partial(work, False), 0)


def shares_of(row, share):
    return row >> (share.bit_length() - 1), row & (share - 1)


def order_rows(found, taken, size, blocks, groups):
    high, low, source, target = found
    return [
        high * 64.0 + low,
        source + (1.0 - taken) * blocks,
        target + (1.0 - taken) * groups,
        0.5 * jnp.sum(size, axis=0, keepdims=True),
    ]


def image_kernel(
    shares, cut, meta, rows_h, cols_h, degree_h, start, tiles,
    own_one, own_two, send,
    acc, rows, cols, degree, panel, order, order_s, held, in_sem, order_sem, tile_sem,
):
    groups = degree.shape[0]
    share = groups // shares
    slots = rows.shape[1]
    places = order.shape[1]
    copies = [
        pltpu.make_async_copy(source, target, in_sem.at[i])
        for i, (source, target) in enumerate(
            ((rows_h, rows), (cols_h, cols), (degree_h, degree), (start, panel.at[pl.ds(0, groups)]))
        )
    ]
    for copy in copies:
        copy.start()
    count, core = meta[0], meta[1]
    copies[0].wait()
    copies[1].wait()
    lane = iota((1, slots), 1)
    row, col = rows[...], cols[...]
    part, at = shares_of(row, share)
    key = jnp.where(at < cut, part * cut + at, shares * cut + part * (share - cut) + at - cut)
    found, taken, size = build_list(
        groups, places, key, lane < count, [lane >> 6, lane & 63, col, key]
    )
    order[...] = pack_rows(order_rows(found, taken, size, groups, groups), places)
    order_copy = pltpu.make_async_copy(order, order_s, order_sem)
    order_copy.start()
    acc[...] = jnp.zeros_like(acc)
    order_copy.wait()

    copies[2].wait()
    copies[3].wait()
    scale = lax.transpose(lax.rsqrt(degree[...]), (1, 0))

    def scale_block(g):
        panel[g] = (panel[g].astype(F32) * scale[:, g : g + 1]).astype(BF16)

    panel[groups] = jnp.zeros(panel.shape[1:], BF16)
    steps = [functools.partial(scale_block, g) for g in range(groups)]
    multiply(False, order_s, order_s[3, 0], groups, tiles, held, tile_sem, panel, acc, steps)
    split_out(acc, 0, shares, cut, core, own_one, send.at[pl.ds(0, own_one.shape[0])])
    split_out(
        acc, shares * cut, shares, share - cut, core, own_two,
        send.at[pl.ds(own_one.shape[0], own_two.shape[0])],
    )


def order_kernel(shares, cut, groups, meta, rows, cols, back_one, back_two):
    share = groups // shares
    slots = rows.shape[1]
    places = back_one.shape[1]
    count, core = meta[0], meta[1]
    lane = iota((1, slots), 1)
    row, col = rows[...], cols[...]
    part, at = shares_of(row, share)
    for out, size, piece, inside in (
        (back_one, cut, at < cut, at),
        (back_two, share - cut, at >= cut, at - cut),
    ):
        blocks = shares * size
        place = ((part & 1) ^ core) * (blocks // 2) + (part >> 1) * size + inside
        found, taken, padded = build_list(
            groups, places, col, (lane < count) & piece, [lane >> 6, lane & 63, place, col]
        )
        out[...] = pack_rows(order_rows(found, taken, padded, blocks, groups), places)


def caption_part(order, tiles, mine, other, acc, panel, held, sem, tile_sem):
    half = mine.shape[0]
    copies = [
        pltpu.make_async_copy(source, panel.at[pl.ds(i * half, half)], sem.at[i])
        for i, source in enumerate((mine, other))
    ]
    for copy in copies:
        copy.start()
    panel[2 * half] = jnp.zeros(panel.shape[1:], BF16)

    def clear(g):
        acc[g] = jnp.zeros(acc.shape[1:], F32)

    steps = [functools.partial(clear, g) for g in range(acc.shape[0])]
    steps += [copy.wait for copy in copies]
    dead = acc.shape[0] - 1
    multiply(True, order, order[3, 0], dead, tiles, held, tile_sem, panel, acc, steps)


def third_kernel(order, tiles, mine, other, out, mark, acc, panel, held, sem, tile_sem):
    mark[...] = jnp.zeros_like(mark)
    caption_part(order, tiles, mine, other, acc, panel, held, sem, tile_sem)

    def block(i, carry):
        out[i] = acc[i].astype(BF16)
        return carry

    lax.fori_loop(0, out.shape[0], block, 0, unroll=4)


def fourth_kernel(
    meta, order, tiles, before, mine, other, own_a, send_a, own_b, send_b,
    acc, panel, held, sem, tile_sem,
):
    caption_part(order, tiles, mine, other, acc, panel, held, sem, tile_sem)
    part = own_a.shape[0]
    for own, send, base, bit in ((own_a, send_a, 0, meta[0]), (own_b, send_b, 2 * part, meta[1])):

        def block(i, carry):
            keep, give = base + bit * part + i, base + (1 - bit) * part + i
            own[i] = acc[keep] + before[keep].astype(F32)
            send[i] = (acc[give] + before[give].astype(F32)).astype(BF16)
            return carry

        lax.fori_loop(0, part, block, 0, unroll=4)


def factor_kernel(root, gram, upper, inverse, rest, left):
    size = gram.shape[0]
    rest[...] = gram[...]
    left[...] = ones_where(iota((size, size), 0) == iota((size, size), 1), F32)
    row = iota((8, size), 0)
    for base in range(0, size, 8):
        panel = pl.ds(base, 8)
        u, m = rest[panel, :], left[panel, :]
        columns = [jnp.broadcast_to(u[:, base + k : base + k + 1], (8, size)) for k in range(8)]
        scale = jnp.zeros((8, size), F32)
        for s in range(8):
            pivot = columns[s][s : s + 1]
            root_of = lax.rsqrt(pivot)
            scale = jnp.where(row == s, root_of, scale)
            f = jnp.where(row > s, columns[s] * (root_of * root_of), 0.0)
            for k in range(s + 1, 8):
                columns[k] = columns[k] - f * columns[k][s : s + 1]
            u = u - f * u[s : s + 1]
            m = m - f * m[s : s + 1]
        u = jnp.where(iota((8, size), 1) >= row + base, u * scale, 0.0)
        m = m * scale
        upper[panel, :] = u * (1.0 / root)
        inverse[panel, :] = m * root
        if base + 8 < size:
            both = lax.dot_general(
                u,
                jnp.concatenate([u, m], axis=1),
                (((0,), (0,)), ((), ())),
                precision=lax.Precision.HIGHEST,
                preferred_element_type=F32,
            )
            rest[...] -= both[:, :size]
            left[...] -= both[:, size:]


VMEM = pl.BlockSpec(memory_space=pltpu.VMEM)
SMEM = pl.BlockSpec(memory_space=pltpu.SMEM)
ANY = pl.BlockSpec(memory_space=pl.ANY)
HBM = pl.BlockSpec(memory_space=pltpu.HBM)
PARAMS = pltpu.CompilerParams(vmem_limit_bytes=32 * 2**20)
DEPTH = 3


def in_hbm(x):
    return pltpu.with_memory_space_constraint(x, pltpu.HBM)


def buffers(tile):
    return [
        pltpu.VMEM((DEPTH * 2 * UNROLL, tile, tile), BF16),
        pltpu.SemaphoreType.DMA((DEPTH,)),
    ]


def places_of(slots, groups):
    return (pl.cdiv(slots + groups, 2 * UNROLL) + 1) * 2 * UNROLL


def forward(shares, cut, meta, rows, cols, degree, start, tiles):
    slots, tile, _ = tiles.shape
    groups, _, width = start.shape
    places = places_of(slots, groups)
    block = (tile, width)
    one = shares // 2 * cut
    two = groups // 2 - one
    held, tile_sem = buffers(tile)
    return pl.pallas_call(
        functools.partial(image_kernel, shares, cut),
        in_specs=[SMEM] + [HBM] * 5,
        out_specs=[VMEM] * 3,
        out_shape=[
            jax.ShapeDtypeStruct((one, *block), F32),
            jax.ShapeDtypeStruct((two, *block), F32),
            jax.ShapeDtypeStruct((one + two, *block), BF16),
        ],
        scratch_shapes=[
            pltpu.VMEM((groups + 1, *block), F32),
            pltpu.VMEM((1, slots), jnp.int32),
            pltpu.VMEM((1, slots), jnp.int32),
            pltpu.VMEM((groups, tile), F32),
            pltpu.VMEM((groups + 1, *block), BF16),
            pltpu.VMEM((8, places), jnp.int32),
            pltpu.SMEM((8, places), jnp.int32),
            held,
            pltpu.SemaphoreType.DMA((4,)),
            pltpu.SemaphoreType.DMA,
            tile_sem,
        ],
        compiler_params=PARAMS,
        name="image",
    )(meta, *map(in_hbm, (rows, cols, degree, start, tiles)))


def back_orders(shares, cut, groups, meta, rows, cols):
    listing = jax.ShapeDtypeStruct((8, places_of(rows.shape[1], groups)), jnp.int32)
    return pl.pallas_call(
        functools.partial(order_kernel, shares, cut, groups),
        in_specs=[SMEM, VMEM, VMEM],
        out_specs=[VMEM] * 2,
        out_shape=[listing] * 2,
        compiler_params=PARAMS,
        name="orders",
    )(meta, rows, cols)


def backward_one(groups, order, tiles, mine, other):
    block = mine.shape[1:]
    held, tile_sem = buffers(block[0])
    return pl.pallas_call(
        third_kernel,
        in_specs=[SMEM, HBM, ANY, ANY],
        out_specs=[VMEM] * 2,
        out_shape=[
            jax.ShapeDtypeStruct((groups, *block), BF16),
            jax.ShapeDtypeStruct((1, 128), F32),
        ],
        scratch_shapes=[
            pltpu.VMEM((groups + 1, *block), F32),
            pltpu.VMEM((2 * mine.shape[0] + 1, *block), BF16),
            held,
            pltpu.SemaphoreType.DMA((2,)),
            tile_sem,
        ],
        compiler_params=PARAMS,
        name="caption_one",
    )(order, in_hbm(tiles), mine, other)


def backward_two(groups, meta, order, tiles, before, mine, other):
    block = mine.shape[1:]
    part = groups // 4
    held, tile_sem = buffers(block[0])
    return pl.pallas_call(
        fourth_kernel,
        in_specs=[SMEM, SMEM, HBM, VMEM, ANY, ANY],
        out_specs=[VMEM] * 4,
        out_shape=[
            jax.ShapeDtypeStruct((part, *block), F32),
            jax.ShapeDtypeStruct((part, *block), BF16),
        ]
        * 2,
        scratch_shapes=[
            pltpu.VMEM((groups + 1, *block), F32),
            pltpu.VMEM((2 * mine.shape[0] + 1, *block), BF16),
            held,
            pltpu.SemaphoreType.DMA((2,)),
            tile_sem,
        ],
        compiler_params=PARAMS,
        name="caption_two",
    )(meta, order, in_hbm(tiles), before, mine, other)


def factorize(gram, root):
    shape = jax.ShapeDtypeStruct(gram.shape, F32)
    return pl.pallas_call(
        functools.partial(factor_kernel, root),
        in_specs=[VMEM],
        out_specs=[VMEM] * 2,
        out_shape=[shape] * 2,
        scratch_shapes=[pltpu.VMEM(gram.shape, F32)] * 2,
        name="factorize",
    )(gram)


def halves(x, bit):
    n = x.shape[0] // 2
    return (
        lax.dynamic_slice_in_dim(x, bit * n, n, 0),
        lax.dynamic_slice_in_dim(x, (1 - bit) * n, n, 0),
    )


def joined(own, other, bit):
    return jnp.where(bit == 0, jnp.concatenate([own, other]), jnp.concatenate([other, own]))


def rounded(x):
    return lax.reduce_precision(x, exponent_bits=8, mantissa_bits=7).astype(BF16)


def in_two(x):
    high = rounded(x)
    return jnp.stack([high, rounded(x - high.astype(F32))])


def from_two(x):
    return x[0].astype(F32) + x[1].astype(F32)


def swap_with(x, extra, axis, bit):
    size = x.shape[0]
    arrived = swap(jnp.concatenate([x, extra]), axis, bit)
    return arrived[:size], in_two(from_two(extra) + from_two(arrived[size:]))


def reduce_rest(own, arrived, bits, extra=None):
    parts = [own, arrived]
    for i, bit in enumerate(bits[1:]):
        if i == len(bits) - 2:
            give = rounded(sum(x.astype(F32) for x in parts))
            parts = [give]
        else:
            split = [halves(x, bit_of("img", bit)) for x in parts]
            give = rounded(sum(x.astype(F32) for _, x in split))
            parts = [x for x, _ in split]
        if extra is None or i > 0:
            arrived = swap(give, "img", bit)
        else:
            arrived, extra = swap_with(give, extra, "img", bit)
        parts.append(arrived)
    return sum(x.astype(F32) for x in parts), extra


def scatter_start(x, bits):
    for bit in bits[:-1]:
        x = halves(x, bit_of("img", bit))[0]
    return x


def gather_back(x, bits, extra=None, along=None):
    for bit in reversed(bits[:-1]):
        if bit == along:
            arrived, extra = swap_with(x, extra, "img", bit)
        else:
            arrived = swap(x, "img", bit)
        x = joined(x, arrived, bit_of("img", bit))
    return x, extra


def body(tile_values, tile_rows, tile_cols, tile_count, row_degree, col_degree, start_panel):
    slots, tile, _ = tile_values.shape
    width = start_panel.shape[1]
    row_total = row_degree.shape[0]
    col_total = col_degree.shape[0]
    row_groups = row_total // tile
    col_groups = col_total // tile
    caps = lax.axis_size("cap")
    imgs = lax.axis_size("img")
    cap_bits = caps.bit_length() - 1
    img_bits = imgs.bit_length() - 1
    core = bit_of("cap", 0)
    chip = lax.axis_index("cap") >> 1
    root = math.sqrt(row_total * imgs)
    share = row_groups // caps
    cut = share // 2
    count = tile_count[0, 0]
    row_scale = (1.0 / jnp.sqrt(row_degree)).reshape(caps // 2, 2, share, tile, 1)
    row_scale = lax.dynamic_index_in_dim(row_scale, core, 1, False)
    col_scale = (1.0 / jnp.sqrt(col_degree)).reshape(col_groups, tile, 1)
    degree = col_degree.reshape(col_groups, tile)
    start = start_panel.reshape(col_groups, tile, width)

    meta = jnp.stack([count, core])
    own_one, own_two, send = forward(
        caps, cut, meta, tile_rows, tile_cols, degree, start, tile_values
    )
    came = swap(send, "cap", 0)
    size = own_one.shape[0]
    first = rounded(own_one + came[:size].astype(F32))
    second = rounded(own_two + came[size:].astype(F32))
    order_one, order_two = back_orders(caps, cut, col_groups, meta, tile_rows, tile_cols)

    def over_chips(part):
        part = part.astype(F32)
        for bit in range(1, cap_bits):
            part = rounded(part)
            part = part.astype(F32) + swap(part, "cap", bit).astype(F32)
        return part

    def finish(part, scale):
        scale = scale.reshape(-1, tile, 1)
        image = part * scale
        mine = (image * scale).astype(BF16)
        return image, mine, swap(mine, "cap", 0)

    def products(image):
        flat = image.reshape(-1, width)
        return jnp.dot(flat.T, flat, precision=lax.Precision.HIGH, preferred_element_type=F32)

    scale_one, scale_two = row_scale[:, :cut], row_scale[:, cut:]
    order_one, scale_one = lax.optimization_barrier((order_one, scale_one))
    first, second = over_chips(first), over_chips(second)
    image_one, mine, other = finish(first, scale_one)
    gram = products(image_one)
    before, mark = backward_one(col_groups, order_one, tile_values, mine, other)
    gram, scale_two = lax.optimization_barrier((gram, scale_two + mark[0, 0]))
    image_two, mine, other = finish(second, scale_two)

    order_a = list(range(img_bits))
    order_b = [1, 0, *range(2, img_bits)]
    own_a, send_a, own_b, send_b = backward_two(
        col_groups,
        jnp.stack([bit_of("img", order_a[0]), bit_of("img", order_b[0])]),
        order_two,
        tile_values,
        before,
        mine,
        other,
    )
    send_a, send_b, image_two = lax.optimization_barrier((send_a, send_b, image_two))
    scale_a, scale_b = col_scale[: col_groups // 2], col_scale[col_groups // 2 :]
    got_a = swap(send_a, "img", order_a[0])
    got_b = swap(send_b, "img", order_b[0])
    gram = gram + products(image_two)
    gram = gram + swap(gram, "cap", 0)
    for bit in range(2, img_bits):
        gram = gram + swap(gram, "img", bit)
    gram = in_two(gram)
    sum_a, gram = reduce_rest(own_a, got_a, order_a, gram)
    sum_b, _ = reduce_rest(own_b, got_b, order_b)
    next_a = (sum_a * scatter_start(scale_a, order_a)).astype(BF16)
    next_b = (sum_b * scatter_start(scale_b, order_b)).astype(BF16)
    next_b, gram = gather_back(next_b, order_b, gram, order_a[0])
    next_a, _ = gather_back(next_a, order_a)
    next_panel = jnp.concatenate([next_a, next_b]).reshape(col_total, width)

    factor, inverse = factorize(from_two(gram), root)
    rows = jnp.concatenate(
        [
            lax.dynamic_index_in_dim(image.reshape(caps // 2, -1, tile, width), chip, 0, False)
            for image in (image_one, image_two)
        ]
    ).reshape(share * tile, width)
    basis = lax.dot_general(
        rows,
        inverse,
        (((1,), (1,)), ((), ())),
        precision=lax.Precision.HIGH,
        preferred_element_type=F32,
    )
    return (basis, factor, next_panel)


def solution(mesh):
    placed = (
        P("img", "cap", None),
        P("img", "cap"),
        P("img", "cap"),
        P("img", "cap"),
        P("img"),
        P("cap"),
        P("cap", None),
    )
    return jax.shard_map(
        body,
        mesh=mesh,
        in_specs=placed,
        out_specs=(P(("img", "cap"), None), P(), P("cap", None)),
        check_vma=False,
    )
```
